32 devices in a mesh: groups: 2 (over x), rows: 16 (over z, y, core).
Axes of the slice: x: 2, y: 2, z: 4, core: 2. Of those that a mesh axis runs over, the one named last changes fastest.
Arguments:
- features: bfloat16 [16384, 128], P(('groups', 'rows')), parts along dimension 0, may hold values from -6 to 6
- block_cols: int32 [1024], P(('groups', 'rows')), parts along dimension 0, may hold values from 0 to 63, as said below
- block_vals: bfloat16 [1024, 128, 128], P(('groups', 'rows')), parts along dimension 0, may hold values from 0 to 1, as said below
- degree: int32 [16384], P(('groups', 'rows')), parts along dimension 0, may hold values from 1 to 1040, as said below
- w_self: bfloat16 [128, 256], replicated, may hold values from -0.5 to 0.5
- w_neigh: bfloat16 [128, 256], replicated, may hold values from -0.5 to 0.5
- cotangent: bfloat16 [16384, 256], P(('groups', 'rows')), parts along dimension 0, may hold values from -6 to 6
Outputs:
- output: bfloat16 [16384, 256], P(('groups', 'rows')), parts along dimension 0
- grad_features: bfloat16 [16384, 128], P(('groups', 'rows')), parts along dimension 0
- grad_self: float32 [256, 256], P('groups'), parts along dimension 0
- grad_neigh: float32 [256, 256], P('groups'), parts along dimension 0
The draws below stay inside these ranges and needn't reach their ends.
There are 2 independent parts, one for each index of `groups`. The reference program is written for one: setup_inputs(seed, part) draws one part's arguments, and reference() takes and returns one part's arrays. A program takes and returns all parts, laid end to end along the dimension named above; an argument that names none is the same for every part. Nothing has to cross between parts.
Inputs may be any that keep to these rules, and one draw needn't show every extreme that they name: `block_cols`: the 32 entries of one device name blocks of exactly 16 owners (the owner of block c holds nodes of blocks c - c % 4 to c - c % 4 + 3), each of these owners named by exactly 2 of that device's entries; a block may be named twice. `block_vals`: each entry is 0 or 1. A node's degree is its row sum of A plus its neighbours outside the batch: 1 to 16 of them for every node but the batch's first two; the second node has no neighbour in the batch and one outside, and the first has degree exactly 1040.
All inputs are finite; a program needn't handle non-finite values.
Results may differ from the reference program's by a relative error of at most 0.0052.
Values may be sent and summed in bfloat16 or wider, within the bound.
A program may use at most 64 MiB of HBM per device.

```python
import jax
import jax.numpy as jnp

F_IN = 128
HID = 256
BLOCK = 128
K = 8
NODE_DEV = 512
NODES = 8192
NODE_BLOCKS = 64
ENTRIES = 512


def block_pattern(key):
    pattern = (jax.random.randint(key, (ENTRIES, BLOCK, BLOCK), 0, 40) == 0).astype(jnp.int32)
    return pattern.at[:K, 1, :].set(0)


def draw_block_cols(key, part):
    key = jax.random.fold_in(key, 11)
    n_dev = NODES // NODE_DEV
    row_blocks = NODE_DEV // BLOCK
    per_dev = row_blocks * K
    slots = max(1, per_dev // n_dev)

    def one_device(dev_key):
        key_owner, key_local, key_order = jax.random.split(dev_key, 3)
        owners = jax.random.permutation(key_owner, n_dev)[:per_dev // slots]
        owners = jnp.repeat(owners, slots)
        local = jax.random.randint(key_local, (per_dev,), 0, row_blocks)
        order = jax.random.permutation(key_order, per_dev)
        return (owners * row_blocks + local)[order].astype(jnp.int32)
    return jax.vmap(one_device)(jax.random.split(key, n_dev)).reshape(-1)


def draw_block_vals(key, part):
    pattern = block_pattern(key)
    return pattern.astype(jnp.float32).astype(jnp.bfloat16)


def draw_degree(key, part):
    pattern = block_pattern(key)
    counts = pattern.reshape(NODE_BLOCKS, K, BLOCK, BLOCK).sum(axis=(1, 3)).reshape(NODES)
    key = jax.random.fold_in(key, 31)
    outside = jax.random.randint(key, (NODES,), 1, 17)
    index = jnp.arange(NODES)
    outside = jnp.where(index == 0, K * BLOCK + 16 - counts[0], outside)
    outside = jnp.where(index == 1, 1, outside)
    return (counts + outside).astype(jnp.int32)


def block_scale(own_key, dims, pieces, least, largest):
    level, own = 1.0, jax.random.fold_in(own_key, 6)
    for axis_at, blocks in pieces:
        heights = jnp.exp(jax.random.uniform(jax.random.fold_in(own, axis_at), (blocks,), jnp.float32, least / len(pieces), largest / len(pieces)))
        level = level * jnp.repeat(heights, dims[axis_at] // blocks).reshape([-1 if axis == axis_at else 1 for axis in range(len(dims))])
    return level


def noise(own_key, extent, deviation, limit, cuts=(), kind=jnp.bfloat16):
    level = block_scale(own_key, extent, cuts, -0.22, 0.18) if cuts else 1.0
    array = jax.random.normal(own_key, extent, jnp.float32) * deviation * level
    return jnp.minimum(jnp.maximum(array, -limit), limit).astype(kind)


def setup_inputs(seed: int = 0, part: int = 0) -> dict:
    seeds = jax.random.split(jax.random.key(seed), 8)
    part_keys = jax.random.split(jax.random.fold_in(seeds[7], part), 8)
    return {
        "features": noise(part_keys[0], (NODES, F_IN), 1.0, 6.0, ((0, 16),)),
        "block_cols": draw_block_cols(jax.random.fold_in(jax.random.fold_in(seeds[7], part), 71), part),
        "block_vals": draw_block_vals(jax.random.fold_in(jax.random.fold_in(seeds[7], part), 71), part),
        "degree": draw_degree(jax.random.fold_in(jax.random.fold_in(seeds[7], part), 71), part),
        "w_self": noise(seeds[4], (F_IN, HID), F_IN ** -0.5, 0.5),
        "w_neigh": noise(seeds[5], (F_IN, HID), F_IN ** -0.5, 0.5),
        "cotangent": noise(part_keys[6], (NODES, HID), 1.0, 6.0, ((0, 16),)),
    }


def reference(features, block_cols, block_vals, degree, w_self, w_neigh, cotangent):
    nodes, width = features.shape
    blocks = nodes // BLOCK
    per_row = block_cols.shape[0] // blocks
    values = block_vals.astype(jnp.float32)
    neighbour = features.reshape(blocks, BLOCK, width)[block_cols].astype(jnp.float32)
    terms = jnp.einsum("bij,bjf->bif", values, neighbour)
    aggregate = terms.reshape(blocks, per_row, BLOCK, width).sum(1).reshape(nodes, width)
    scale = degree.astype(jnp.float32)[:, None]
    mean = (aggregate / scale).astype(jnp.bfloat16)
    pre = jnp.dot(features, w_self, preferred_element_type=jnp.float32) + jnp.dot(mean, w_neigh, preferred_element_type=jnp.float32)
    sigma = jax.nn.sigmoid(pre)
    output = (pre * sigma).astype(jnp.bfloat16)
    dpre = (cotangent.astype(jnp.float32) * sigma * (1.0 + pre * (1.0 - sigma))).astype(jnp.bfloat16)
    factor = NODES ** -0.5
    grad_self = jnp.dot(features.T, dpre, preferred_element_type=jnp.float32) * factor
    grad_neigh = jnp.dot(mean.T, dpre, preferred_element_type=jnp.float32) * factor
    dagg = (jnp.dot(dpre, w_neigh.T, preferred_element_type=jnp.float32) / scale).astype(jnp.bfloat16)
    dagg_blocks = jnp.repeat(dagg.reshape(blocks, BLOCK, width).astype(jnp.float32), per_row, axis=0)
    back = jnp.einsum("bji,bjf->bif", values, dagg_blocks)
    spread = jax.ops.segment_sum(back, block_cols, num_segments=blocks).reshape(nodes, width)
    grad_features = (jnp.dot(dpre, w_self.T, preferred_element_type=jnp.float32) + spread).astype(jnp.bfloat16)
    return output, grad_features, grad_self, grad_neigh
```

```python
import functools

import jax
import jax.numpy as jnp
from jax import lax
from jax.experimental import pallas as pl
from jax.experimental.pallas import tpu as pltpu
from jax.sharding import PartitionSpec as P

B = 128
F32 = jnp.float32
BF16 = jnp.bfloat16
NT = (((1,), (1,)), ((), ()))


def remote(src, dst, send, recv, device):
    return pltpu.make_async_remote_copy(
        src_ref=src,
        dst_ref=dst,
        send_sem=send,
        recv_sem=recv,
        device_id={"rows": device},
        device_id_type=pl.DeviceIdType.MESH,
    )


class Place:
    def __init__(self, z_size, y_size):
        self.Z, self.Y = z_size, y_size
        me = lax.axis_index("rows")
        self.me = me
        self.c = me % 2
        self.y = (me // 2) % y_size
        self.z = me // (2 * y_size)
        self.has_down = self.z > 0
        self.has_up = self.z < z_size - 1

    def index(self, z, y, c):
        return (z * self.Y + y) * 2 + c

    @property
    def up(self):
        return self.index(jnp.minimum(self.z + 1, self.Z - 1), self.y, self.c)

    @property
    def down(self):
        return self.index(jnp.maximum(self.z - 1, 0), self.y, self.c)

    @property
    def across(self):
        return self.index(self.z, (self.y + 1) % self.Y, self.c)

    @property
    def sibling(self):
        return self.index(self.z, self.y, 1 - self.c)

    def by_distance(self, k):
        if k == 0:
            return [(None, self.z)]
        return [
            (self.z + k < self.Z, jnp.minimum(self.z + k, self.Z - 1)),
            (self.z - k >= 0, jnp.maximum(self.z - k, 0)),
        ]


def when(cond):
    if cond is None:
        return lambda f: f()
    return pl.when(cond)


class Gather:
    def __init__(self, place, first, buf, chunks, send, recv):
        self.p, self.first, self.buf = place, first, buf
        self.chunks, self.send, self.recv = chunks, send, recv
        self.blocks = buf.shape[0] // (2 * place.Z * place.Y)
        self.part = self.blocks // chunks

    def copy(self, kind, z, y, h, device, own=False):
        piece = self.p.index(z, y, self.p.c)
        dst = self.buf.at[pl.ds(piece * self.blocks + h * self.part, self.part)]
        src = dst
        if own and self.first is not None:
            src = self.first.at[pl.ds(h * self.part, self.part)]
        return remote(
            src, dst, self.send.at[kind, z, h], self.recv.at[kind, z, h], device
        )

    def arrived(self, kind, z, y, h, c=None):
        piece = self.p.index(z, y, self.p.c if c is None else c)
        dst = self.buf.at[pl.ds(piece * self.blocks + h * self.part, self.part)]
        remote(
            dst, dst, self.send.at[kind, z, h], self.recv.at[kind, z, h], self.p.sibling
        ).wait_recv()

    def run(self):
        p = self.p
        for h in range(self.chunks):
            pl.when(p.has_up)(lambda: self.copy(0, p.z, p.y, h, p.up, True).start())
            pl.when(p.has_down)(lambda: self.copy(1, p.z, p.y, h, p.down, True).start())
            if p.Y > 1:
                self.copy(2, p.z, p.y, h, p.across, True).start()
        for h in range(self.chunks):
            self.copy(3 + p.y, p.z, p.y, h, p.sibling, True).start()
        yield
        for k in range(1, p.Z + 1):
            for h in range(self.chunks):
                if k < p.Z:
                    for kind, cond, z in (
                        (0, p.z - k >= 0, jnp.maximum(p.z - k, 0)),
                        (1, p.z + k < p.Z, jnp.minimum(p.z + k, p.Z - 1)),
                    ):

                        @pl.when(cond)
                        def _():
                            self.arrived(kind, z, p.y, h)
                            on, target = ((p.has_up, p.up), (p.has_down, p.down))[kind]
                            pl.when(on)(lambda: self.copy(kind, z, p.y, h, target).start())
                            if p.Y > 1:
                                self.copy(2, z, p.y, h, p.across).start()
                            self.copy(3 + p.y, z, p.y, h, p.sibling).start()

                if p.Y > 1:
                    for cond, z in p.by_distance(k - 1):

                        @when(cond)
                        def _():
                            self.arrived(2, z, 1 - p.y, h)
                            self.copy(4 - p.y, z, 1 - p.y, h, p.sibling).start()

            yield
        for z in range(p.Z):
            for y in range(p.Y):
                for h in range(self.chunks):
                    self.arrived(3 + y, z, y, h, 1 - p.c)
        yield

    def finish(self):
        p = self.p
        for z in range(p.Z):
            for h in range(self.chunks):
                pl.when(p.has_up & (z <= p.z))(
                    lambda: self.copy(0, z, p.y, h, p.up).wait_send()
                )
                pl.when(p.has_down & (z >= p.z))(
                    lambda: self.copy(1, z, p.y, h, p.down).wait_send()
                )
                if p.Y > 1:
                    self.copy(2, z, p.y, h, p.across).wait_send()
                for y in range(p.Y):
                    self.copy(3 + y, z, y, h, p.sibling).wait_send()


class Reduce:
    def __init__(self, place, total, from_core, from_y, from_z, chunks, send, recv):
        self.p, self.total = place, total
        self.from_core, self.from_y, self.from_z = from_core, from_y, from_z
        self.chunks, self.send, self.recv = chunks, send, recv
        self.rows = total.shape[1] // chunks

    def copy(self, kind, z, y, c, h, device):
        rows = pl.ds(h * self.rows, self.rows)
        if kind is None:
            kind, dst = 3 + y, self.from_core.at[y, z, rows]
        elif kind == 2:
            dst = self.from_y.at[z, rows]
        else:
            dst = self.from_z.at[kind, z, rows]
        src = self.total.at[self.p.index(z, y, c), rows]
        return remote(
            src, dst, self.send.at[kind, z, h], self.recv.at[kind, z, h], device
        )

    def take(self, kind, z, y, h):
        p = self.p
        copy = self.copy(kind, z, y, p.c, h, p.sibling)
        copy.wait_recv()
        rows = pl.ds(h * self.rows, self.rows)
        if kind is None:
            term = self.from_core[y, z, rows]
        elif kind == 2:
            term = self.from_y[z, rows]
        else:
            term = self.from_z[kind, z, rows]
        return term.astype(F32)

    def add(self, kinds, z, y, h):
        rows = pl.ds(h * self.rows, self.rows)
        piece = self.p.index(z, y, self.p.c)
        value = self.total[piece, rows].astype(F32)
        for kind in kinds:
            value = value + self.take(kind, z, y, h)
        self.total[piece, rows] = value.astype(self.total.dtype)

    def core_send(self, z, y):
        for h in range(self.chunks):
            self.copy(None, z, y, 1 - self.p.c, h, self.p.sibling).start()

    def stage_y(self):
        p = self.p
        if p.Y == 1:
            return
        for k in range(p.Z - 1, -1, -1):
            for cond, z in p.by_distance(k):

                @when(cond)
                def _():
                    for h in range(self.chunks):
                        self.add([None], z, 1 - p.y, h)
                        self.copy(2, z, 1 - p.y, p.c, h, p.across).start()

    def stage_z(self):
        p = self.p
        near = [None] + ([2] if p.Y > 1 else [])
        for k in range(p.Z - 1, 0, -1):
            for h in range(self.chunks):
                for (cond, z), kind in zip(p.by_distance(k), (0, 1)):

                    @pl.when(cond)
                    def _():
                        self.add(near, z, p.y, h)
                        before = (p.has_down, p.has_up)[kind]
                        pl.when(before)(lambda: self.add([kind], z, p.y, h))
                        self.copy(kind, z, p.y, p.c, h, (p.up, p.down)[kind]).start()

            yield
        for h in range(self.chunks):
            self.add(near, p.z, p.y, h)
            pl.when(p.has_down)(lambda: self.add([0], p.z, p.y, h))
            pl.when(p.has_up)(lambda: self.add([1], p.z, p.y, h))
        yield

    def finish(self):
        p = self.p
        for z in range(p.Z):
            for h in range(self.chunks):
                pl.when(z > p.z)(lambda: self.copy(0, z, p.y, p.c, h, p.up).wait_send())
                pl.when(z < p.z)(lambda: self.copy(1, z, p.y, p.c, h, p.down).wait_send())
                if p.Y > 1:
                    self.copy(2, z, 1 - p.y, p.c, h, p.across).wait_send()
                for y in range(p.Y):
                    self.copy(None, z, y, 1 - p.c, h, p.sibling).wait_send()


def kernel(
    cfg,
    cols,
    table,
    features,
    vals,
    degree,
    w_self,
    w_neigh,
    cotangent,
    output,
    grad_features,
    grad_self,
    grad_neigh,
    everything,
    vals_t,
    dagg,
    total,
    core_in,
    y_in,
    z_in,
    w_total,
    w_core_in,
    w_y_in,
    w_z_in,
    w_all,
    g_send,
    g_recv,
    r_send,
    r_recv,
    wr_send,
    wr_recv,
    wg_send,
    wg_recv,
):
    Z, Y, chunks, per_row, factor = cfg
    p = Place(Z, Y)
    row_blocks, _, width = features.shape
    entries = vals.shape[0]
    n = 2 * Y * Z

    barrier = pltpu.get_barrier_semaphore()

    def greet(device):
        pl.semaphore_signal(
            barrier, inc=1, device_id={"rows": device}, device_id_type=pl.DeviceIdType.MESH
        )

    greet(p.sibling)
    if Y > 1:
        greet(p.across)
    pl.when(p.has_up)(lambda: greet(p.up))
    pl.when(p.has_down)(lambda: greet(p.down))
    ends = (p.z > 0).astype(jnp.int32) + (p.z < Z - 1).astype(jnp.int32)
    pl.semaphore_wait(barrier, (2 if Y > 1 else 1) + ends)

    gather = Gather(p, features, everything, chunks, g_send, g_recv)
    steps = gather.run()
    next(steps)

    for i in range(row_blocks):
        everything[p.me * row_blocks + i] = features[i]
    next(steps)

    per = entries // Z if Z <= entries else 0

    def flip(e, _):
        vals_t[e] = vals[e].T
        return 0

    for k in range(1, Z):
        if per:
            lax.fori_loop((k - 1) * per, k * per, flip, 0)
        next(steps)
    lax.fori_loop((Z - 1) * per, entries, flip, 0)
    vals_t[entries] = jnp.zeros((B, B), BF16)
    dagg[row_blocks] = jnp.zeros((B, width), BF16)
    scales = [
        jnp.broadcast_to(degree[r : r + 1, :].astype(F32), (B, B)).T for r in range(row_blocks)
    ]
    for _ in steps:
        pass

    means, dpres, owns = [], [], []
    for r in range(row_blocks):
        rows = slice(r * B, (r + 1) * B)
        left = jnp.concatenate([vals[r * per_row + j] for j in range(per_row)], axis=1)
        right = jnp.concatenate(
            [everything[cols[r * per_row + j]] for j in range(per_row)], axis=0
        )
        aggregate = jnp.dot(left, right, preferred_element_type=F32)
        mean = (aggregate / scales[r]).astype(BF16)
        own = features[r]
        pre = jnp.dot(own, w_self[...], preferred_element_type=F32) + jnp.dot(
            mean, w_neigh[...], preferred_element_type=F32
        )
        sigma = 1.0 / (1.0 + jnp.exp(-pre))
        output[rows, :] = (pre * sigma).astype(BF16)
        dpre = (cotangent[rows, :].astype(F32) * sigma * (1.0 + pre * (1.0 - sigma))).astype(BF16)
        back = lax.dot_general(dpre, w_neigh[...], NT, preferred_element_type=F32)
        dagg[r] = (back / scales[r]).astype(BF16)
        means.append(mean)
        dpres.append(dpre)
        owns.append(lax.dot_general(dpre, w_self[...], NT, preferred_element_type=F32))

    left = jnp.concatenate(
        [
            jnp.concatenate([features[r] for r in range(row_blocks)], axis=0).T,
            jnp.concatenate(means, axis=0).T,
        ],
        axis=0,
    )
    sums = jnp.dot(left, jnp.concatenate(dpres, axis=0), preferred_element_type=F32)
    w_rows = w_total.shape[1]
    for d in range(n):
        at = d * w_rows
        half, row = divmod(at, 2 * width)
        w_total[d] = sums[row : row + w_rows, half * 128 : half * 128 + 128].astype(w_total.dtype)
    w_sum = Reduce(p, w_total, w_core_in, w_y_in, w_z_in, 1, wr_send, wr_recv)
    for z in range(Z):
        for y in range(Y):
            w_sum.core_send(z, y)

    spread = Reduce(p, total, core_in, y_in, z_in, chunks, r_send, r_recv)

    def spread_piece(piece):
        for b in range(row_blocks):
            block = piece * row_blocks + b
            one, two = table[0, block], table[1, block]
            left = jnp.concatenate([vals_t[one], vals_t[two]], axis=1)
            right = jnp.concatenate([dagg[table[2, block]], dagg[table[3, block]]], axis=0)
            total[piece, b * B : (b + 1) * B] = jnp.dot(
                left, right, preferred_element_type=F32
            ).astype(BF16)

    def order(i):
        z = jnp.where(p.z < Z // 2, p.z + Z - 1 - i, p.z + 1 + i) % Z
        return z

    def for_sibling(i, _):
        y = (i % Y + p.y + 1) % Y
        z = order(i // Y)
        spread_piece(p.index(z, y, 1 - p.c))
        spread.core_send(z, y)
        return 0

    def for_own(i, _):
        spread_piece(p.index(i // Y, i % Y, p.c))
        return 0

    lax.fori_loop(0, Z * Y, for_sibling, 0)
    w_sum.stage_y()
    lax.fori_loop(0, Z * Y, for_own, 0)
    spread.stage_y()

    for _ in w_sum.stage_z():
        pass
    w_all[p.me] = w_total[p.me]
    w_gather = Gather(p, None, w_all, 1, wg_send, wg_recv)
    w_steps = w_gather.run()
    next(w_steps)
    for _ in spread.stage_z():
        next(w_steps, None)
    for r in range(row_blocks):
        rows = slice(r * B, (r + 1) * B)
        grad_features[rows, :] = (owns[r] + total[p.me, rows].astype(F32)).astype(BF16)
    for _ in w_steps:
        pass
    for d in range(n):
        at = d * w_rows
        half, row = divmod(at, 2 * width)
        target, row = ((grad_self, row), (grad_neigh, row - width))[row // width]
        target[row : row + w_rows, half * 128 : half * 128 + 128] = w_all[d].astype(F32) * factor

    gather.finish()
    w_sum.finish()
    spread.finish()
    w_gather.finish()


def body(Z, Y, features, block_cols, block_vals, degree, w_self, w_neigh, cotangent):
    nodes, width = features.shape
    hidden = w_self.shape[1]
    entries = block_cols.shape[0]
    row_blocks = nodes // B
    n = 2 * Y * Z
    blocks = n * row_blocks
    chunks = 2 if Z <= 4 else 1
    number = jnp.arange(entries, dtype=jnp.int32)[None, :]
    match = block_cols[None, :] == jnp.arange(blocks, dtype=jnp.int32)[:, None]
    first = jnp.min(jnp.where(match, number, entries), axis=1)
    last = jnp.max(jnp.where(match, number, -1), axis=1)
    last = jnp.where((last == first) | (last < 0), entries, last)
    per_row = entries // row_blocks
    table = jnp.stack([first, last, first // per_row, last // per_row])

    w_rows = 4 * width * hidden // 256 // n
    w_type = BF16 if w_rows % 16 == 0 else F32
    cfg = (Z, Y, chunks, entries // row_blocks, float(nodes * n) ** -0.5)
    vmem = pl.BlockSpec(memory_space=pltpu.VMEM)
    smem = pl.BlockSpec(memory_space=pltpu.SMEM)

    def sems(chunks):
        return [pltpu.SemaphoreType.DMA((3 + Y, Z, chunks))] * 2

    return pl.pallas_call(
        functools.partial(kernel, cfg),
        out_shape=(
            jax.ShapeDtypeStruct((nodes, hidden), BF16),
            jax.ShapeDtypeStruct((nodes, width), BF16),
            jax.ShapeDtypeStruct((width, hidden), F32),
            jax.ShapeDtypeStruct((width, hidden), F32),
        ),
        in_specs=[smem, smem] + [vmem] * 6,
        out_specs=[vmem] * 4,
        scratch_shapes=[
            pltpu.VMEM((blocks, B, width), BF16),
            pltpu.VMEM((entries + 1, B, B), BF16),
            pltpu.VMEM((row_blocks + 1, B, width), BF16),
            pltpu.VMEM((n, nodes, width), BF16),
            pltpu.VMEM((Y, Z, nodes, width), BF16),
            pltpu.VMEM((Z if Y > 1 else 1, nodes, width), BF16),
            pltpu.VMEM((2, Z, nodes, width), BF16),
            pltpu.VMEM((n, w_rows, 128), w_type),
            pltpu.VMEM((Y, Z, w_rows, 128), w_type),
            pltpu.VMEM((Z, w_rows, 128), w_type),
            pltpu.VMEM((2, Z, w_rows, 128), w_type),
            pltpu.VMEM((n, w_rows, 128), w_type),
        ]
        + sems(chunks)
        + sems(chunks)
        + sems(1)
        + sems(1),
        compiler_params=pltpu.CompilerParams(
            collective_id=0, has_side_effects=True, vmem_limit_bytes=56 * 1024 * 1024
        ),
        cost_estimate=pl.CostEstimate(
            flops=600_000_000, bytes_accessed=4_000_000, transcendentals=131072
        ),
    )(
        block_cols,
        table,
        features.reshape(row_blocks, B, width),
        block_vals,
        degree.reshape(row_blocks, B),
        w_self,
        w_neigh,
        cotangent,
    )


def solution(mesh):
    rows = mesh.shape["rows"]
    Y = 2 if rows <= 16 and rows % 4 == 0 else 1
    Z = rows // (2 * Y)
    return jax.shard_map(
        functools.partial(body, Z, Y),
        mesh=mesh,
        in_specs=(
            P(("groups", "rows"), None),
            P(("groups", "rows")),
            P(("groups", "rows"), None, None),
            P(("groups", "rows")),
            P(),
            P(),
            P(("groups", "rows"), None),
        ),
        out_specs=(
            P(("groups", "rows"), None),
            P(("groups", "rows"), None),
            P("groups", None),
            P("groups", None),
        ),
        check_vma=False,
    )
```

```python
import functools

import jax
import jax.numpy as jnp
from jax import lax
from jax.experimental import pallas as pl
from jax.experimental.pallas import tpu as pltpu
from jax.sharding import PartitionSpec as P

B = 128
F32 = jnp.float32
BF16 = jnp.bfloat16
NT = (((1,), (1,)), ((), ()))


def remote(src, dst, send, recv, device):
    return pltpu.make_async_remote_copy(
        src_ref=src,
        dst_ref=dst,
        send_sem=send,
        recv_sem=recv,
        device_id={"rows": device},
        device_id_type=pl.DeviceIdType.MESH,
    )


class Place:
    def __init__(self, z_size, y_size):
        self.Z, self.Y = z_size, y_size
        me = lax.axis_index("rows")
        self.me = me
        self.c = me % 2
        self.y = (me // 2) % y_size
        self.z = me // (2 * y_size)
        self.has_down = self.z > 0
        self.has_up = self.z < z_size - 1

    def index(self, z, y, c):
        return (z * self.Y + y) * 2 + c

    @property
    def up(self):
        return self.index(jnp.minimum(self.z + 1, self.Z - 1), self.y, self.c)

    @property
    def down(self):
        return self.index(jnp.maximum(self.z - 1, 0), self.y, self.c)

    @property
    def across(self):
        return self.index(self.z, (self.y + 1) % self.Y, self.c)

    @property
    def sibling(self):
        return self.index(self.z, self.y, 1 - self.c)

    def by_distance(self, k):
        if k == 0:
            return [(None, self.z)]
        return [
            (self.z + k < self.Z, jnp.minimum(self.z + k, self.Z - 1)),
            (self.z - k >= 0, jnp.maximum(self.z - k, 0)),
        ]


def when(cond):
    if cond is None:
        return lambda f: f()
    return pl.when(cond)


class Gather:
    def __init__(self, place, first, buf, chunks, send, recv):
        self.p, self.first, self.buf = place, first, buf
        self.chunks, self.send, self.recv = chunks, send, recv
        self.blocks = buf.shape[0] // (2 * place.Z * place.Y)
        self.part = self.blocks // chunks

    def copy(self, kind, z, y, h, device, own=False):
        piece = self.p.index(z, y, self.p.c)
        dst = self.buf.at[pl.ds(piece * self.blocks + h * self.part, self.part)]
        src = dst
        if own and self.first is not None:
            src = self.first.at[pl.ds(h * self.part, self.part)]
        return remote(
            src, dst, self.send.at[kind, z, h], self.recv.at[kind, z, h], device
        )

    def arrived(self, kind, z, y, h, c=None):
        piece = self.p.index(z, y, self.p.c if c is None else c)
        dst = self.buf.at[pl.ds(piece * self.blocks + h * self.part, self.part)]
        remote(
            dst, dst, self.send.at[kind, z, h], self.recv.at[kind, z, h], self.p.sibling
        ).wait_recv()

    def run(self):
        p = self.p
        for h in range(self.chunks):
            pl.when(p.has_up)(lambda: self.copy(0, p.z, p.y, h, p.up, True).start())
            pl.when(p.has_down)(lambda: self.copy(1, p.z, p.y, h, p.down, True).start())
            if p.Y > 1:
                self.copy(2, p.z, p.y, h, p.across, True).start()
        for h in range(self.chunks):
            self.copy(3 + p.y, p.z, p.y, h, p.sibling, True).start()
        yield
        for k in range(1, p.Z + 1):
            for h in range(self.chunks):
                if k < p.Z:
                    for kind, cond, z in (
                        (0, p.z - k >= 0, jnp.maximum(p.z - k, 0)),
                        (1, p.z + k < p.Z, jnp.minimum(p.z + k, p.Z - 1)),
                    ):

                        @pl.when(cond)
                        def _():
                            self.arrived(kind, z, p.y, h)
                            on, target = ((p.has_up, p.up), (p.has_down, p.down))[kind]
                            pl.when(on)(lambda: self.copy(kind, z, p.y, h, target).start())
                            if p.Y > 1:
                                self.copy(2, z, p.y, h, p.across).start()
                            self.copy(3 + p.y, z, p.y, h, p.sibling).start()

                if p.Y > 1:
                    for cond, z in p.by_distance(k - 1):

                        @when(cond)
                        def _():
                            self.arrived(2, z, 1 - p.y, h)
                            self.copy(4 - p.y, z, 1 - p.y, h, p.sibling).start()

            yield
        for z in range(p.Z):
            for y in range(p.Y):
                for h in range(self.chunks):
                    self.arrived(3 + y, z, y, h, 1 - p.c)
        yield

    def finish(self):
        p = self.p
        for z in range(p.Z):
            for h in range(self.chunks):
                pl.when(p.has_up & (z <= p.z))(
                    lambda: self.copy(0, z, p.y, h, p.up).wait_send()
                )
                pl.when(p.has_down & (z >= p.z))(
                    lambda: self.copy(1, z, p.y, h, p.down).wait_send()
                )
                if p.Y > 1:
                    self.copy(2, z, p.y, h, p.across).wait_send()
                for y in range(p.Y):
                    self.copy(3 + y, z, y, h, p.sibling).wait_send()


class Reduce:
    def __init__(self, place, total, from_core, from_y, from_z, chunks, send, recv):
        self.p, self.total = place, total
        self.from_core, self.from_y, self.from_z = from_core, from_y, from_z
        self.chunks, self.send, self.recv = chunks, send, recv
        self.rows = total.shape[1] // chunks

    def copy(self, kind, z, y, c, h, device):
        rows = pl.ds(h * self.rows, self.rows)
        if kind is None:
            kind, dst = 3 + y, self.from_core.at[y, z, rows]
        elif kind == 2:
            dst = self.from_y.at[z, rows]
        else:
            dst = self.from_z.at[kind, z, rows]
        src = self.total.at[self.p.index(z, y, c), rows]
        return remote(
            src, dst, self.send.at[kind, z, h], self.recv.at[kind, z, h], device
        )

    def take(self, kind, z, y, h):
        p = self.p
        copy = self.copy(kind, z, y, p.c, h, p.sibling)
        copy.wait_recv()
        rows = pl.ds(h * self.rows, self.rows)
        if kind is None:
            term = self.from_core[y, z, rows]
        elif kind == 2:
            term = self.from_y[z, rows]
        else:
            term = self.from_z[kind, z, rows]
        return term.astype(F32)

    def add(self, kinds, z, y, h):
        rows = pl.ds(h * self.rows, self.rows)
        piece = self.p.index(z, y, self.p.c)
        value = self.total[piece, rows].astype(F32)
        for kind in kinds:
            value = value + self.take(kind, z, y, h)
        self.total[piece, rows] = value.astype(self.total.dtype)

    def core_send(self, z, y):
        for h in range(self.chunks):
            self.copy(None, z, y, 1 - self.p.c, h, self.p.sibling).start()

    def stage_y(self):
        p = self.p
        if p.Y == 1:
            return
        for k in range(p.Z - 1, -1, -1):
            for cond, z in p.by_distance(k):

                @when(cond)
                def _():
                    for h in range(self.chunks):
                        self.add([None], z, 1 - p.y, h)
                        self.copy(2, z, 1 - p.y, p.c, h, p.across).start()

    def stage_z(self):
        p = self.p
        near = [None] + ([2] if p.Y > 1 else [])
        for k in range(p.Z - 1, 0, -1):
            for h in range(self.chunks):
                for (cond, z), kind in zip(p.by_distance(k), (0, 1)):

                    @pl.when(cond)
                    def _():
                        self.add(near, z, p.y, h)
                        before = (p.has_down, p.has_up)[kind]
                        pl.when(before)(lambda: self.add([kind], z, p.y, h))
                        self.copy(kind, z, p.y, p.c, h, (p.up, p.down)[kind]).start()

            yield
        for h in range(self.chunks):
            self.add(near, p.z, p.y, h)
            pl.when(p.has_down)(lambda: self.add([0], p.z, p.y, h))
            pl.when(p.has_up)(lambda: self.add([1], p.z, p.y, h))
        yield

    def finish(self):
        p = self.p
        for z in range(p.Z):
            for h in range(self.chunks):
                pl.when(z > p.z)(lambda: self.copy(0, z, p.y, p.c, h, p.up).wait_send())
                pl.when(z < p.z)(lambda: self.copy(1, z, p.y, p.c, h, p.down).wait_send())
                if p.Y > 1:
                    self.copy(2, z, 1 - p.y, p.c, h, p.across).wait_send()
                for y in range(p.Y):
                    self.copy(None, z, y, 1 - p.c, h, p.sibling).wait_send()


def kernel(
    cfg,
    cols,
    table,
    features,
    vals_hbm,
    degree,
    w_self,
    w_neigh,
    cotangent_hbm,
    output_hbm,
    grad_features,
    grad_self,
    grad_neigh,
    everything,
    vals_t,
    dagg,
    total,
    core_in,
    y_in,
    z_in,
    w_total,
    w_core_in,
    w_y_in,
    w_z_in,
    w_all,
    g_send,
    g_recv,
    r_send,
    r_recv,
    wr_send,
    wr_recv,
    wg_send,
    wg_recv,
    vals,
    cotangent,
    output,
    local,
):
    Z, Y, chunks, per_row, factor = cfg
    p = Place(Z, Y)
    row_blocks, _, width = features.shape
    entries = vals.shape[0]
    vals_in = pltpu.make_async_copy(vals_hbm, vals, local.at[0])
    cotangent_in = pltpu.make_async_copy(cotangent_hbm, cotangent, local.at[1])
    output_out = pltpu.make_async_copy(output, output_hbm, local.at[2])
    vals_in.start()
    cotangent_in.start()
    n = 2 * Y * Z

    barrier = pltpu.get_barrier_semaphore()

    def greet(device):
        pl.semaphore_signal(
            barrier, inc=1, device_id={"rows": device}, device_id_type=pl.DeviceIdType.MESH
        )

    greet(p.sibling)
    if Y > 1:
        greet(p.across)
    pl.when(p.has_up)(lambda: greet(p.up))
    pl.when(p.has_down)(lambda: greet(p.down))
    ends = (p.z > 0).astype(jnp.int32) + (p.z < Z - 1).astype(jnp.int32)
    pl.semaphore_wait(barrier, (2 if Y > 1 else 1) + ends)

    gather = Gather(p, features, everything, chunks, g_send, g_recv)
    steps = gather.run()
    next(steps)

    for i in range(row_blocks):
        everything[p.me * row_blocks + i] = features[i]
    vals_in.wait()
    cotangent_in.wait()
    next(steps)

    per = entries // Z if Z <= entries else 0

    def flip(e, _):
        vals_t[e] = vals[e].T
        return 0

    for k in range(1, Z):
        if per:
            lax.fori_loop((k - 1) * per, k * per, flip, 0)
        next(steps)
    lax.fori_loop((Z - 1) * per, entries, flip, 0)
    vals_t[entries] = jnp.zeros((B, B), BF16)
    dagg[row_blocks] = jnp.zeros((B, width), BF16)
    scales = [
        jnp.broadcast_to(degree[r : r + 1, :].astype(F32), (B, B)).T for r in range(row_blocks)
    ]
    for _ in steps:
        pass

    means, dpres, owns = [], [], []
    for r in range(row_blocks):
        rows = slice(r * B, (r + 1) * B)
        left = jnp.concatenate([vals[r * per_row + j] for j in range(per_row)], axis=1)
        right = jnp.concatenate(
            [everything[cols[r * per_row + j]] for j in range(per_row)], axis=0
        )
        aggregate = jnp.dot(left, right, preferred_element_type=F32)
        mean = (aggregate / scales[r]).astype(BF16)
        own = features[r]
        pre = jnp.dot(own, w_self[...], preferred_element_type=F32) + jnp.dot(
            mean, w_neigh[...], preferred_element_type=F32
        )
        sigma = 1.0 / (1.0 + jnp.exp(-pre))
        output[rows, :] = (pre * sigma).astype(BF16)
        dpre = (cotangent[rows, :].astype(F32) * sigma * (1.0 + pre * (1.0 - sigma))).astype(BF16)
        back = lax.dot_general(dpre, w_neigh[...], NT, preferred_element_type=F32)
        dagg[r] = (back / scales[r]).astype(BF16)
        means.append(mean)
        dpres.append(dpre)
        owns.append(lax.dot_general(dpre, w_self[...], NT, preferred_element_type=F32))

    output_out.start()

    left = jnp.concatenate(
        [
            jnp.concatenate([features[r] for r in range(row_blocks)], axis=0).T,
            jnp.concatenate(means, axis=0).T,
        ],
        axis=0,
    )
    sums = jnp.dot(left, jnp.concatenate(dpres, axis=0), preferred_element_type=F32)
    w_rows = w_total.shape[1]
    for d in range(n):
        at = d * w_rows
        half, row = divmod(at, 2 * width)
        w_total[d] = sums[row : row + w_rows, half * 128 : half * 128 + 128].astype(w_total.dtype)
    w_sum = Reduce(p, w_total, w_core_in, w_y_in, w_z_in, 1, wr_send, wr_recv)
    for z in range(Z):
        for y in range(Y):
            w_sum.core_send(z, y)

    spread = Reduce(p, total, core_in, y_in, z_in, chunks, r_send, r_recv)

    def spread_piece(piece):
        for b in range(row_blocks):
            block = piece * row_blocks + b
            one, two = table[0, block], table[1, block]
            left = jnp.concatenate([vals_t[one], vals_t[two]], axis=1)
            right = jnp.concatenate([dagg[table[2, block]], dagg[table[3, block]]], axis=0)
            total[piece, b * B : (b + 1) * B] = jnp.dot(
                left, right, preferred_element_type=F32
            ).astype(BF16)

    def order(i):
        z = jnp.where(p.z < Z // 2, p.z + Z - 1 - i, p.z + 1 + i) % Z
        return z

    def for_sibling(i, _):
        y = (i % Y + p.y + 1) % Y
        z = order(i // Y)
        spread_piece(p.index(z, y, 1 - p.c))
        spread.core_send(z, y)
        return 0

    def for_own(i, _):
        spread_piece(p.index(i // Y, i % Y, p.c))
        return 0

    lax.fori_loop(0, Z * Y, for_sibling, 0)
    w_sum.stage_y()
    lax.fori_loop(0, Z * Y, for_own, 0)
    spread.stage_y()

    w_steps, t_steps = w_sum.stage_z(), spread.stage_z()
    next(w_steps)
    next(t_steps)
    for _ in w_steps:
        pass
    w_all[p.me] = w_total[p.me]

    def hand(i, source):
        mine = w_all.at[source]
        return remote(mine, mine, wg_send.at[i], wg_recv.at[i], (p.me + i) % n)

    def hand_start(i, _):
        hand(i, p.me).start()
        return 0

    def hand_wait(i, _):
        hand(i, (p.me + n - i) % n).wait_recv()
        return 0

    def hand_finish(i, _):
        hand(i, p.me).wait_send()
        return 0

    lax.fori_loop(1, n, hand_start, 0)
    for _ in t_steps:
        pass
    for r in range(row_blocks):
        rows = slice(r * B, (r + 1) * B)
        grad_features[rows, :] = (owns[r] + total[p.me, rows].astype(F32)).astype(BF16)
    lax.fori_loop(1, n, hand_wait, 0)
    for d in range(n):
        at = d * w_rows
        half, row = divmod(at, 2 * width)
        target, row = ((grad_self, row), (grad_neigh, row - width))[row // width]
        target[row : row + w_rows, half * 128 : half * 128 + 128] = w_all[d].astype(F32) * factor

    output_out.wait()
    gather.finish()
    w_sum.finish()
    spread.finish()
    lax.fori_loop(1, n, hand_finish, 0)


def hand_over(a, b, c, d, a_out, b_out, c_out, d_out, sems):
    pairs = ((a, a_out), (b, b_out), (c, c_out), (d, d_out))
    copies = [pltpu.make_async_copy(x, y, sems.at[i]) for i, (x, y) in enumerate(pairs)]
    for copy in copies:
        copy.start()
    for copy in copies:
        copy.wait()


def body(Z, Y, features, block_cols, block_vals, degree, w_self, w_neigh, cotangent):
    nodes, width = features.shape
    hidden = w_self.shape[1]
    entries = block_cols.shape[0]
    row_blocks = nodes // B
    n = 2 * Y * Z
    blocks = n * row_blocks
    chunks = 2 if Z <= 4 else 1
    number = jnp.arange(entries, dtype=jnp.int32)[None, :]
    match = block_cols[None, :] == jnp.arange(blocks, dtype=jnp.int32)[:, None]
    first = jnp.min(jnp.where(match, number, entries), axis=1)
    last = jnp.max(jnp.where(match, number, -1), axis=1)
    last = jnp.where((last == first) | (last < 0), entries, last)
    per_row = entries // row_blocks
    table = jnp.stack([first, last, first // per_row, last // per_row])

    w_rows = 4 * width * hidden // 256 // n
    w_type = BF16 if w_rows % 16 == 0 else F32
    cfg = (Z, Y, chunks, entries // row_blocks, float(nodes * n) ** -0.5)
    vmem = pl.BlockSpec(memory_space=pltpu.VMEM)
    smem = pl.BlockSpec(memory_space=pltpu.SMEM)
    hbm = pl.BlockSpec(memory_space=pl.ANY)

    def sems(chunks):
        return [pltpu.SemaphoreType.DMA((3 + Y, Z, chunks))] * 2

    results = pl.pallas_call(
        functools.partial(kernel, cfg),
        out_shape=(
            jax.ShapeDtypeStruct((nodes, hidden), BF16),
            jax.ShapeDtypeStruct((nodes, width), BF16),
            jax.ShapeDtypeStruct((width, hidden), F32),
            jax.ShapeDtypeStruct((width, hidden), F32),
        ),
        in_specs=[smem, smem, vmem, hbm, vmem, vmem, vmem, hbm],
        out_specs=[hbm, vmem, vmem, vmem],
        scratch_shapes=[
            pltpu.VMEM((blocks, B, width), BF16),
            pltpu.VMEM((entries + 1, B, B), BF16),
            pltpu.VMEM((row_blocks + 1, B, width), BF16),
            pltpu.VMEM((n, nodes, width), BF16),
            pltpu.VMEM((Y, Z, nodes, width), BF16),
            pltpu.VMEM((Z if Y > 1 else 1, nodes, width), BF16),
            pltpu.VMEM((2, Z, nodes, width), BF16),
            pltpu.VMEM((n, w_rows, 128), w_type),
            pltpu.VMEM((Y, Z, w_rows, 128), w_type),
            pltpu.VMEM((Z, w_rows, 128), w_type),
            pltpu.VMEM((2, Z, w_rows, 128), w_type),
            pltpu.VMEM((n, w_rows, 128), w_type),
        ]
        + sems(chunks)
        + sems(chunks)
        + sems(1)
        + [pltpu.SemaphoreType.DMA((n,))] * 2
        + [
            pltpu.VMEM((entries, B, B), BF16),
            pltpu.VMEM((nodes, hidden), BF16),
            pltpu.VMEM((nodes, hidden), BF16),
            pltpu.SemaphoreType.DMA((3,)),
        ],
        compiler_params=pltpu.CompilerParams(
            collective_id=0, has_side_effects=True, vmem_limit_bytes=56 * 1024 * 1024
        ),
        cost_estimate=pl.CostEstimate(
            flops=600_000_000, bytes_accessed=4_000_000, transcendentals=131072
        ),
    )(
        block_cols,
        table,
        features.reshape(row_blocks, B, width),
        block_vals,
        degree.reshape(row_blocks, B),
        w_self,
        w_neigh,
        cotangent,
    )
    anywhere = pl.BlockSpec(memory_space=pl.ANY)
    return pl.pallas_call(
        hand_over,
        out_shape=tuple(jax.ShapeDtypeStruct(x.shape, x.dtype) for x in results),
        in_specs=[pl.BlockSpec(memory_space=pltpu.VMEM)] * 4,
        out_specs=[anywhere] * 4,
        scratch_shapes=[pltpu.SemaphoreType.DMA((4,))],
    )(*results)


def solution(mesh):
    rows = mesh.shape["rows"]
    Y = 2 if rows <= 16 and rows % 4 == 0 else 1
    Z = rows // (2 * Y)
    return jax.shard_map(
        functools.partial(body, Z, Y),
        mesh=mesh,
        in_specs=(
            P(("groups", "rows"), None),
            P(("groups", "rows")),
            P(("groups", "rows"), None, None),
            P(("groups", "rows")),
            P(),
            P(),
            P(("groups", "rows"), None),
        ),
        out_specs=(
            P(("groups", "rows"), None),
            P(("groups", "rows"), None),
            P("groups", None),
            P("groups", None),
        ),
        check_vma=False,
    )
```

```python
import functools

import jax
import jax.numpy as jnp
from jax import lax
from jax.experimental import pallas as pl
from jax.experimental.pallas import tpu as pltpu
from jax.sharding import PartitionSpec as P

B = 128
F32 = jnp.float32
BF16 = jnp.bfloat16
NT = (((1,), (1,)), ((), ()))


def remote(src, dst, send, recv, device):
    return pltpu.make_async_remote_copy(
        src_ref=src,
        dst_ref=dst,
        send_sem=send,
        recv_sem=recv,
        device_id={"rows": device},
        device_id_type=pl.DeviceIdType.MESH,
    )


class Place:
    def __init__(self, z_size, y_size):
        self.Z, self.Y = z_size, y_size
        me = lax.axis_index("rows")
        self.me = me
        self.c = me % 2
        self.y = (me // 2) % y_size
        self.z = me // (2 * y_size)
        self.has_down = self.z > 0
        self.has_up = self.z < z_size - 1

    def index(self, z, y, c):
        return (z * self.Y + y) * 2 + c

    @property
    def up(self):
        return self.index(jnp.minimum(self.z + 1, self.Z - 1), self.y, self.c)

    @property
    def down(self):
        return self.index(jnp.maximum(self.z - 1, 0), self.y, self.c)

    @property
    def across(self):
        return self.index(self.z, (self.y + 1) % self.Y, self.c)

    @property
    def sibling(self):
        return self.index(self.z, self.y, 1 - self.c)

    def by_distance(self, k):
        if k == 0:
            return [(None, self.z)]
        return [
            (self.z + k < self.Z, jnp.minimum(self.z + k, self.Z - 1)),
            (self.z - k >= 0, jnp.maximum(self.z - k, 0)),
        ]


def when(cond):
    if cond is None:
        return lambda f: f()
    return pl.when(cond)


class Gather:
    def __init__(self, place, first, buf, chunks, send, recv):
        self.p, self.first, self.buf = place, first, buf
        self.chunks, self.send, self.recv = chunks, send, recv
        self.blocks = buf.shape[0] // (2 * place.Z * place.Y)
        self.part = self.blocks // chunks

    def copy(self, kind, z, y, h, device, own=False):
        piece = self.p.index(z, y, self.p.c)
        dst = self.buf.at[pl.ds(piece * self.blocks + h * self.part, self.part)]
        src = dst
        if own and self.first is not None:
            src = self.first.at[pl.ds(h * self.part, self.part)]
        return remote(
            src, dst, self.send.at[kind, z, h], self.recv.at[kind, z, h], device
        )

    def arrived(self, kind, z, y, h, c=None):
        piece = self.p.index(z, y, self.p.c if c is None else c)
        dst = self.buf.at[pl.ds(piece * self.blocks + h * self.part, self.part)]
        remote(
            dst, dst, self.send.at[kind, z, h], self.recv.at[kind, z, h], self.p.sibling
        ).wait_recv()

    def run(self):
        p = self.p
        for h in range(self.chunks):
            pl.when(p.has_up)(lambda: self.copy(0, p.z, p.y, h, p.up, True).start())
            pl.when(p.has_down)(lambda: self.copy(1, p.z, p.y, h, p.down, True).start())
            if p.Y > 1:
                self.copy(2, p.z, p.y, h, p.across, True).start()
        for h in range(self.chunks):
            self.copy(3 + p.y, p.z, p.y, h, p.sibling, True).start()
        yield
        for k in range(1, p.Z + 1):
            for h in range(self.chunks):
                if k < p.Z:
                    for kind, cond, z in (
                        (0, p.z - k >= 0, jnp.maximum(p.z - k, 0)),
                        (1, p.z + k < p.Z, jnp.minimum(p.z + k, p.Z - 1)),
                    ):

                        @pl.when(cond)
                        def _():
                            self.arrived(kind, z, p.y, h)
                            on, target = ((p.has_up, p.up), (p.has_down, p.down))[kind]
                            pl.when(on)(lambda: self.copy(kind, z, p.y, h, target).start())
                            if p.Y > 1:
                                self.copy(2, z, p.y, h, p.across).start()
                            self.copy(3 + p.y, z, p.y, h, p.sibling).start()

                if p.Y > 1:
                    for cond, z in p.by_distance(k - 1):

                        @when(cond)
                        def _():
                            self.arrived(2, z, 1 - p.y, h)
                            self.copy(4 - p.y, z, 1 - p.y, h, p.sibling).start()

            yield
        for z in range(p.Z):
            for y in range(p.Y):
                for h in range(self.chunks):
                    self.arrived(3 + y, z, y, h, 1 - p.c)
        yield

    def finish(self):
        p = self.p
        for z in range(p.Z):
            for h in range(self.chunks):
                pl.when(p.has_up & (z <= p.z))(
                    lambda: self.copy(0, z, p.y, h, p.up).wait_send()
                )
                pl.when(p.has_down & (z >= p.z))(
                    lambda: self.copy(1, z, p.y, h, p.down).wait_send()
                )
                if p.Y > 1:
                    self.copy(2, z, p.y, h, p.across).wait_send()
                for y in range(p.Y):
                    self.copy(3 + y, z, y, h, p.sibling).wait_send()


class Reduce:
    def __init__(self, place, total, from_core, from_y, from_z, chunks, send, recv):
        self.p, self.total = place, total
        self.from_core, self.from_y, self.from_z = from_core, from_y, from_z
        self.chunks, self.send, self.recv = chunks, send, recv
        self.rows = total.shape[1] // chunks

    def copy(self, kind, z, y, c, h, device):
        rows = pl.ds(h * self.rows, self.rows)
        if kind is None:
            kind, dst = 3 + y, self.from_core.at[y, z, rows]
        elif kind == 2:
            dst = self.from_y.at[z, rows]
        else:
            dst = self.from_z.at[kind, z, rows]
        src = self.total.at[self.p.index(z, y, c), rows]
        return remote(
            src, dst, self.send.at[kind, z, h], self.recv.at[kind, z, h], device
        )

    def take(self, kind, z, y, h):
        p = self.p
        copy = self.copy(kind, z, y, p.c, h, p.sibling)
        copy.wait_recv()
        rows = pl.ds(h * self.rows, self.rows)
        if kind is None:
            term = self.from_core[y, z, rows]
        elif kind == 2:
            term = self.from_y[z, rows]
        else:
            term = self.from_z[kind, z, rows]
        return term.astype(F32)

    def add(self, kinds, z, y, h):
        rows = pl.ds(h * self.rows, self.rows)
        piece = self.p.index(z, y, self.p.c)
        value = self.total[piece, rows].astype(F32)
        for kind in kinds:
            value = value + self.take(kind, z, y, h)
        self.total[piece, rows] = value.astype(self.total.dtype)

    def core_send(self, z, y):
        for h in range(self.chunks):
            self.copy(None, z, y, 1 - self.p.c, h, self.p.sibling).start()

    def stage_y(self):
        p = self.p
        if p.Y == 1:
            return
        for k in range(p.Z - 1, -1, -1):
            for cond, z in p.by_distance(k):

                @when(cond)
                def _():
                    for h in range(self.chunks):
                        self.add([None], z, 1 - p.y, h)
                        self.copy(2, z, 1 - p.y, p.c, h, p.across).start()

    def stage_z(self):
        p = self.p
        near = [None] + ([2] if p.Y > 1 else [])
        for k in range(p.Z - 1, 0, -1):
            for h in range(self.chunks):
                for (cond, z), kind in zip(p.by_distance(k), (0, 1)):

                    @pl.when(cond)
                    def _():
                        self.add(near, z, p.y, h)
                        before = (p.has_down, p.has_up)[kind]
                        pl.when(before)(lambda: self.add([kind], z, p.y, h))
                        self.copy(kind, z, p.y, p.c, h, (p.up, p.down)[kind]).start()

            yield
        for h in range(self.chunks):
            self.add(near, p.z, p.y, h)
            pl.when(p.has_down)(lambda: self.add([0], p.z, p.y, h))
            pl.when(p.has_up)(lambda: self.add([1], p.z, p.y, h))
        yield

    def finish(self):
        p = self.p
        for z in range(p.Z):
            for h in range(self.chunks):
                pl.when(z > p.z)(lambda: self.copy(0, z, p.y, p.c, h, p.up).wait_send())
                pl.when(z < p.z)(lambda: self.copy(1, z, p.y, p.c, h, p.down).wait_send())
                if p.Y > 1:
                    self.copy(2, z, 1 - p.y, p.c, h, p.across).wait_send()
                for y in range(p.Y):
                    self.copy(None, z, y, 1 - p.c, h, p.sibling).wait_send()


def kernel(
    cfg,
    cols,
    table,
    features,
    vals_hbm,
    degree,
    w_self,
    w_neigh,
    cotangent_hbm,
    output_hbm,
    grad_features,
    grad_self,
    grad_neigh,
    everything,
    vals_t,
    dagg,
    total,
    core_in,
    y_in,
    z_in,
    w_total,
    w_core_in,
    w_y_in,
    w_z_in,
    w_all,
    g_send,
    g_recv,
    r_send,
    r_recv,
    wr_send,
    wr_recv,
    wg_send,
    wg_recv,
    vals,
    cotangent,
    output,
    local,
):
    Z, Y, chunks, per_row, factor = cfg
    p = Place(Z, Y)
    row_blocks, _, width = features.shape
    entries = vals.shape[0]
    vals_in = pltpu.make_async_copy(vals_hbm, vals, local.at[0])
    cotangent_in = pltpu.make_async_copy(cotangent_hbm, cotangent, local.at[1])
    output_out = pltpu.make_async_copy(output, output_hbm, local.at[2])
    vals_in.start()
    cotangent_in.start()
    n = 2 * Y * Z

    barrier = pltpu.get_barrier_semaphore()

    def greet(device):
        pl.semaphore_signal(
            barrier, inc=1, device_id={"rows": device}, device_id_type=pl.DeviceIdType.MESH
        )

    greet(p.sibling)
    if Y > 1:
        greet(p.across)
    pl.when(p.has_up)(lambda: greet(p.up))
    pl.when(p.has_down)(lambda: greet(p.down))
    ends = (p.z > 0).astype(jnp.int32) + (p.z < Z - 1).astype(jnp.int32)
    pl.semaphore_wait(barrier, (2 if Y > 1 else 1) + ends)

    gather = Gather(p, features, everything, chunks, g_send, g_recv)
    steps = gather.run()
    next(steps)

    for i in range(row_blocks):
        everything[p.me * row_blocks + i] = features[i]
    vals_in.wait()
    cotangent_in.wait()
    next(steps)

    per = entries // Z if Z <= entries else 0

    def flip(e, _):
        vals_t[e] = vals[e].T
        return 0

    for k in range(1, Z):
        if per:
            lax.fori_loop((k - 1) * per, k * per, flip, 0)
        next(steps)
    lax.fori_loop((Z - 1) * per, entries, flip, 0)
    vals_t[entries] = jnp.zeros((B, B), BF16)
    dagg[row_blocks] = jnp.zeros((B, width), BF16)
    scales = [
        jnp.broadcast_to(degree[r : r + 1, :].astype(F32), (B, B)).T for r in range(row_blocks)
    ]
    for _ in steps:
        pass

    means, dpres, owns = [], [], []
    for r in range(row_blocks):
        rows = slice(r * B, (r + 1) * B)
        left = jnp.concatenate([vals[r * per_row + j] for j in range(per_row)], axis=1)
        right = jnp.concatenate(
            [everything[cols[r * per_row + j]] for j in range(per_row)], axis=0
        )
        aggregate = jnp.dot(left, right, preferred_element_type=F32)
        mean = (aggregate / scales[r]).astype(BF16)
        own = features[r]
        pre = jnp.dot(own, w_self[...], preferred_element_type=F32) + jnp.dot(
            mean, w_neigh[...], preferred_element_type=F32
        )
        sigma = 1.0 / (1.0 + jnp.exp(-pre))
        output[rows, :] = (pre * sigma).astype(BF16)
        dpre = (cotangent[rows, :].astype(F32) * sigma * (1.0 + pre * (1.0 - sigma))).astype(BF16)
        back = lax.dot_general(dpre, w_neigh[...], NT, preferred_element_type=F32)
        dagg[r] = (back / scales[r]).astype(BF16)
        means.append(mean)
        dpres.append(dpre)
        owns.append(lax.dot_general(dpre, w_self[...], NT, preferred_element_type=F32))

    output_out.start()

    left = jnp.concatenate(
        [
            jnp.concatenate([features[r] for r in range(row_blocks)], axis=0).T,
            jnp.concatenate(means, axis=0).T,
        ],
        axis=0,
    )
    sums = jnp.dot(left, jnp.concatenate(dpres, axis=0), preferred_element_type=F32)
    w_rows = w_total.shape[3]
    for d in range(n):
        at = d * w_rows
        half, row = divmod(at, 2 * width)
        w_total[d % 2, d // 2 % Y, d // 2 // Y] = sums[row : row + w_rows, half * 128 : half * 128 + 128].astype(w_total.dtype)
    w_type = w_total.dtype
    w_core = remote(
        w_total.at[1 - p.c], w_core_in, wr_send.at[3, 0, 0], wr_recv.at[3, 0, 0], p.sibling
    )
    w_y = remote(
        w_total.at[p.c, (p.y + 1) % Y], w_y_in, wr_send.at[2, 0, 0], wr_recv.at[2, 0, 0], p.across
    )

    def w_z(kind, z):
        return remote(
            w_total.at[p.c, p.y, z],
            w_z_in.at[kind, z],
            wr_send.at[kind, z, 0],
            wr_recv.at[kind, z, 0],
            (p.up, p.down)[kind],
        )

    def w_add(kind, z):
        remote(
            w_z_in.at[kind, z],
            w_z_in.at[kind, z],
            wr_send.at[kind, z, 0],
            wr_recv.at[kind, z, 0],
            p.sibling,
        ).wait_recv()
        value = w_total[p.c, p.y, z].astype(F32) + w_z_in[kind, z].astype(F32)
        w_total[p.c, p.y, z] = value.astype(w_type)

    def w_stage_z():
        if Y > 1:
            w_y.wait_recv()
            value = w_total[p.c, p.y].astype(F32) + w_y_in[...].astype(F32)
            w_total[p.c, p.y] = value.astype(w_type)
        for k in range(Z - 1, 0, -1):
            for (cond, z), kind in zip(p.by_distance(k), (0, 1)):

                @pl.when(cond)
                def _():
                    before = (p.has_down, p.has_up)[kind]
                    pl.when(before)(lambda: w_add(kind, z))
                    w_z(kind, z).start()

            yield
        pl.when(p.has_down)(lambda: w_add(0, p.z))
        pl.when(p.has_up)(lambda: w_add(1, p.z))
        yield

    w_core.start()

    spread = Reduce(p, total, core_in, y_in, z_in, chunks, r_send, r_recv)

    def spread_piece(piece):
        for b in range(row_blocks):
            block = piece * row_blocks + b
            one, two = table[0, block], table[1, block]
            left = jnp.concatenate([vals_t[one], vals_t[two]], axis=1)
            right = jnp.concatenate([dagg[table[2, block]], dagg[table[3, block]]], axis=0)
            total[piece, b * B : (b + 1) * B] = jnp.dot(
                left, right, preferred_element_type=F32
            ).astype(BF16)

    def order(i):
        z = jnp.where(p.z < Z // 2, p.z + Z - 1 - i, p.z + 1 + i) % Z
        return z

    def for_sibling(i, _):
        y = (i % Y + p.y + 1) % Y
        z = order(i // Y)
        spread_piece(p.index(z, y, 1 - p.c))
        spread.core_send(z, y)
        return 0

    def for_own(i, _):
        spread_piece(p.index(i // Y, i % Y, p.c))
        return 0

    lax.fori_loop(0, Z * Y, for_sibling, 0)
    w_core.wait_recv()
    w_total[p.c] = (w_total[p.c].astype(F32) + w_core_in[...].astype(F32)).astype(w_type)
    if Y > 1:
        w_y.start()
    lax.fori_loop(0, Z * Y, for_own, 0)
    spread.stage_y()

    w_steps, t_steps = w_stage_z(), spread.stage_z()
    next(w_steps)
    next(t_steps)
    for _ in w_steps:
        pass
    w_all[p.me] = w_total[p.c, p.y, p.z]

    def hand(i, source):
        mine = w_all.at[source]
        return remote(mine, mine, wg_send.at[i], wg_recv.at[i], (p.me + i) % n)

    def hand_start(i, _):
        hand(i, p.me).start()
        return 0

    def hand_wait(i, _):
        hand(i, (p.me + n - i) % n).wait_recv()
        return 0

    def hand_finish(i, _):
        hand(i, p.me).wait_send()
        return 0

    lax.fori_loop(1, n, hand_start, 0)
    for _ in t_steps:
        pass
    for r in range(row_blocks):
        rows = slice(r * B, (r + 1) * B)
        grad_features[rows, :] = (owns[r] + total[p.me, rows].astype(F32)).astype(BF16)
    lax.fori_loop(1, n, hand_wait, 0)
    for d in range(n):
        at = d * w_rows
        half, row = divmod(at, 2 * width)
        target, row = ((grad_self, row), (grad_neigh, row - width))[row // width]
        target[row : row + w_rows, half * 128 : half * 128 + 128] = w_all[d].astype(F32) * factor

    output_out.wait()
    gather.finish()
    w_core.wait_send()
    if Y > 1:
        w_y.wait_send()
    for z in range(Z):
        pl.when(z > p.z)(lambda: w_z(0, z).wait_send())
        pl.when(z < p.z)(lambda: w_z(1, z).wait_send())
    spread.finish()
    lax.fori_loop(1, n, hand_finish, 0)


def hand_over(a, b, c, d, a_out, b_out, c_out, d_out, sems):
    pairs = ((a, a_out), (b, b_out), (c, c_out), (d, d_out))
    copies = [pltpu.make_async_copy(x, y, sems.at[i]) for i, (x, y) in enumerate(pairs)]
    for copy in copies:
        copy.start()
    for copy in copies:
        copy.wait()


def body(Z, Y, features, block_cols, block_vals, degree, w_self, w_neigh, cotangent):
    nodes, width = features.shape
    hidden = w_self.shape[1]
    entries = block_cols.shape[0]
    row_blocks = nodes // B
    n = 2 * Y * Z
    blocks = n * row_blocks
    chunks = 2 if Z <= 4 else 1
    number = jnp.arange(entries, dtype=jnp.int32)[None, :]
    match = block_cols[None, :] == jnp.arange(blocks, dtype=jnp.int32)[:, None]
    first = jnp.min(jnp.where(match, number, entries), axis=1)
    last = jnp.max(jnp.where(match, number, -1), axis=1)
    last = jnp.where((last == first) | (last < 0), entries, last)
    per_row = entries // row_blocks
    table = jnp.stack([first, last, first // per_row, last // per_row])

    w_rows = 4 * width * hidden // 256 // n
    w_type = BF16 if w_rows % 16 == 0 else F32
    cfg = (Z, Y, chunks, entries // row_blocks, float(nodes * n) ** -0.5)
    vmem = pl.BlockSpec(memory_space=pltpu.VMEM)
    smem = pl.BlockSpec(memory_space=pltpu.SMEM)
    hbm = pl.BlockSpec(memory_space=pl.ANY)

    def sems(chunks):
        return [pltpu.SemaphoreType.DMA((3 + Y, Z, chunks))] * 2

    results = pl.pallas_call(
        functools.partial(kernel, cfg),
        out_shape=(
            jax.ShapeDtypeStruct((nodes, hidden), BF16),
            jax.ShapeDtypeStruct((nodes, width), BF16),
            jax.ShapeDtypeStruct((width, hidden), F32),
            jax.ShapeDtypeStruct((width, hidden), F32),
        ),
        in_specs=[smem, smem, vmem, hbm, vmem, vmem, vmem, hbm],
        out_specs=[hbm, vmem, vmem, vmem],
        scratch_shapes=[
            pltpu.VMEM((blocks, B, width), BF16),
            pltpu.VMEM((entries + 1, B, B), BF16),
            pltpu.VMEM((row_blocks + 1, B, width), BF16),
            pltpu.VMEM((n, nodes, width), BF16),
            pltpu.VMEM((Y, Z, nodes, width), BF16),
            pltpu.VMEM((Z if Y > 1 else 1, nodes, width), BF16),
            pltpu.VMEM((2, Z, nodes, width), BF16),
            pltpu.VMEM((2, Y, Z, w_rows, 128), w_type),
            pltpu.VMEM((Y, Z, w_rows, 128), w_type),
            pltpu.VMEM((Z, w_rows, 128), w_type),
            pltpu.VMEM((2, Z, w_rows, 128), w_type),
            pltpu.VMEM((n, w_rows, 128), w_type),
        ]
        + sems(chunks)
        + sems(chunks)
        + sems(1)
        + [pltpu.SemaphoreType.DMA((n,))] * 2
        + [
            pltpu.VMEM((entries, B, B), BF16),
            pltpu.VMEM((nodes, hidden), BF16),
            pltpu.VMEM((nodes, hidden), BF16),
            pltpu.SemaphoreType.DMA((3,)),
        ],
        compiler_params=pltpu.CompilerParams(
            collective_id=0, has_side_effects=True, vmem_limit_bytes=56 * 1024 * 1024
        ),
        cost_estimate=pl.CostEstimate(
            flops=600_000_000, bytes_accessed=4_000_000, transcendentals=131072
        ),
    )(
        block_cols,
        table,
        features.reshape(row_blocks, B, width),
        block_vals,
        degree.reshape(row_blocks, B),
        w_self,
        w_neigh,
        cotangent,
    )
    anywhere = pl.BlockSpec(memory_space=pl.ANY)
    return pl.pallas_call(
        hand_over,
        out_shape=tuple(jax.ShapeDtypeStruct(x.shape, x.dtype) for x in results),
        in_specs=[pl.BlockSpec(memory_space=pltpu.VMEM)] * 4,
        out_specs=[anywhere] * 4,
        scratch_shapes=[pltpu.SemaphoreType.DMA((4,))],
    )(*results)


def solution(mesh):
    rows = mesh.shape["rows"]
    Y = 2 if rows <= 16 and rows % 4 == 0 else 1
    Z = rows // (2 * Y)
    return jax.shard_map(
        functools.partial(body, Z, Y),
        mesh=mesh,
        in_specs=(
            P(("groups", "rows"), None),
            P(("groups", "rows")),
            P(("groups", "rows"), None, None),
            P(("groups", "rows")),
            P(),
            P(),
            P(("groups", "rows"), None),
        ),
        out_specs=(
            P(("groups", "rows"), None),
            P(("groups", "rows"), None),
            P("groups", None),
            P("groups", None),
        ),
        check_vma=False,
    )
```
